512 devices in a mesh: ctx: 64 (over z, x, core), tp: 8 (over y).
Axes of the slice: x: 4, y: 8, z: 8, core: 2. Of those that a mesh axis runs over, the one named last changes fastest.
Arguments:
- queries: bfloat16 [32768, 4096], P('ctx', 'tp'), may hold values from -6 to 6
- keys: bfloat16 [32768, 4096], P('ctx', 'tp'), may hold values from -6 to 6
- values: bfloat16 [32768, 4096], P('ctx', 'tp'), may hold values from -6 to 6
- out_weight: bfloat16 [4096, 4096], P('tp', 'ctx'), may hold values from -0.09375 to 0.09375
Outputs:
- mixed: bfloat16 [32768, 4096], P(('ctx', 'tp'))
The draws below stay inside these ranges and needn't reach their ends.
All inputs are finite; a program needn't handle non-finite values.
Results may differ from the reference program's by a relative error of at most 0.018.
Values may be sent and summed in bfloat16 or wider, within the bound.
No kernel may reach another device: no remote copies, remote signals or barrier semaphores. Data moves between devices by JAX's collectives and lax.ppermute only.
A program may use at most 64 MiB of HBM per device.

```python
import jax
import jax.numpy as jnp
from jax import lax

D = 4096
HEADS = 32
HD = 128
BLK = 512
TOKENS = 32768
N_TP = 8


def block_levels(own_key, shape, cuts, low, largest):
    loudness, own = 1.0, jax.random.fold_in(own_key, 6)
    for axis_at, shards_of in cuts:
        draws = jnp.exp(jax.random.uniform(jax.random.fold_in(own, axis_at), (shards_of,), jnp.float32, low / len(cuts), largest / len(cuts)))
        loudness = loudness * jnp.repeat(draws, shape[axis_at] // shards_of).reshape([-1 if axis == axis_at else 1 for axis in range(len(shape))])
    return loudness


def noise(rng, shape, scale, bound, pieces=(), dtype=jnp.bfloat16):
    array = scale * jax.random.normal(rng, shape, jnp.float32)
    if pieces:
        array = array * block_levels(rng, shape, pieces, -0.22, 0.18)
    return jnp.clip(array, -bound, bound).astype(dtype)


def setup_inputs(seed: int = 0) -> dict:
    arg_keys = jax.random.split(jax.random.key(seed), 5)
    queries = noise(arg_keys[0], (TOKENS, HEADS * HD), 1.0, 6.0, ((0, 64), (1, 8)))
    keys = noise(arg_keys[1], (TOKENS, HEADS * HD), 1.0, 6.0, ((0, 64), (1, 8)))
    values = noise(arg_keys[2], (TOKENS, HEADS * HD), 1.0, 6.0, ((0, 64), (1, 8)))
    out_weight = noise(arg_keys[3], (HEADS * HD, D), (HEADS * HD) ** -0.5, 0.09375, ((0, 8), (1, 64)))
    return {"queries": queries, "keys": keys, "values": values, "out_weight": out_weight}


def reference(queries, keys, values, out_weight):
    blocks = TOKENS // BLK
    shape = (blocks, BLK, HEADS, HD)
    qb = queries.reshape(shape)
    kb = keys.reshape(shape)
    vb = values.reshape(shape)
    causal = jnp.arange(BLK)[:, None] >= jnp.arange(BLK)[None, :]

    def step(state, items):
        q_blk, k_blk, v_blk = items
        carried = state.astype(jnp.bfloat16)
        inter = jnp.einsum('thd,hde->the', q_blk.astype(jnp.float32), carried.astype(jnp.float32))
        scores = jnp.einsum('thd,shd->hts', q_blk.astype(jnp.float32), k_blk.astype(jnp.float32))
        scores = jnp.where(causal[None], scores, 0.0).astype(jnp.bfloat16)
        intra = jnp.einsum('hts,she->the', scores.astype(jnp.float32), v_blk.astype(jnp.float32))
        attended = inter + intra
        normed = attended / jnp.sqrt(lax.optimization_barrier(jnp.mean(attended * attended, axis=-1, keepdims=True)) + 1e-06)
        block_state = jnp.einsum('thd,the->hde', k_blk.astype(jnp.float32), v_blk.astype(jnp.float32))
        return (state + block_state, normed.astype(jnp.bfloat16))
    start = jnp.zeros((HEADS, HD, HD), jnp.float32)
    _, normed = lax.scan(step, start, (qb, kb, vb))
    normed = normed.reshape(TOKENS, HEADS * HD)
    group = HEADS * HD // N_TP
    total = jnp.zeros((TOKENS, D), jnp.float32)
    for index in range(N_TP):
        part_rows = normed[:, index * group:(index + 1) * group]
        weight_rows = out_weight[index * group:(index + 1) * group]
        partial_g = jnp.dot(part_rows, weight_rows, preferred_element_type=jnp.float32).astype(jnp.bfloat16)
        total = total + partial_g.astype(jnp.float32)
    return total.astype(jnp.bfloat16)
```

```python
import jax
import jax.numpy as jnp
from jax import lax
from jax.experimental import pallas as pl
from jax.experimental.pallas import tpu as pltpu
from jax.sharding import Mesh, PartitionSpec as P

HD = 128
F32 = jnp.float32
BF16 = jnp.bfloat16
Z, X, C, Y = 8, 4, 2, 8


def state_kernel(k_ref, v_ref, s_ref):
    for h in range(4):
        cols = slice(h * HD, (h + 1) * HD)
        s = lax.dot_general(
            k_ref[:, cols], v_ref[:, cols], (((0,), (0,)), ((), ())), preferred_element_type=F32
        )
        s_ref[cols, :] = s.astype(BF16)


def states(keys, values):
    return pl.pallas_call(
        state_kernel,
        out_shape=jax.ShapeDtypeStruct((4 * HD, HD), BF16),
        compiler_params=pltpu.CompilerParams(vmem_limit_bytes=16 * 2**20),
        cost_estimate=pl.CostEstimate(flops=2 * 512 * 512 * 128, bytes_accessed=2**20, transcendentals=0),
    )(keys, values)


def attention_kernel(q_ref, k_ref, v_ref, c_ref, o_ref):
    half = 256
    row = lax.broadcasted_iota(jnp.int32, (half, half), 0)
    col = lax.broadcasted_iota(jnp.int32, (half, half), 1)
    causal = row >= col
    nt = (((1,), (1,)), ((), ()))

    def masked(q, k):
        s = lax.dot_general(q, k, nt, preferred_element_type=F32)
        return jnp.where(causal, s, 0.0).astype(BF16)

    def norm(a):
        r = lax.rsqrt(jnp.mean(a * a, axis=-1, keepdims=True) + 1e-06)
        return (a * r).astype(BF16)

    c = c_ref[...]
    q0, q1 = q_ref[:half], q_ref[half:]
    k0, k1 = k_ref[:half], k_ref[half:]
    v0, v1 = v_ref[:half], v_ref[half:]
    a0 = jnp.dot(q0, c, preferred_element_type=F32)
    a0 += jnp.dot(masked(q0, k0), v0, preferred_element_type=F32)
    o_ref[:half] = norm(a0)
    a1 = jnp.dot(q1, c, preferred_element_type=F32)
    s10 = lax.dot_general(q1, k0, nt, preferred_element_type=F32).astype(BF16)
    a1 += jnp.dot(s10, v0, preferred_element_type=F32)
    a1 += jnp.dot(masked(q1, k1), v1, preferred_element_type=F32)
    o_ref[half:] = norm(a1)


def attention(queries, keys, values, carried):
    by_head = pl.BlockSpec((512, HD), lambda h: (0, h))
    return pl.pallas_call(
        attention_kernel,
        grid=(4,),
        in_specs=[by_head, by_head, by_head, pl.BlockSpec((HD, HD), lambda h: (h, 0))],
        out_specs=by_head,
        out_shape=jax.ShapeDtypeStruct((512, 512), BF16),
        compiler_params=pltpu.CompilerParams(vmem_limit_bytes=24 * 2**20),
        cost_estimate=pl.CostEstimate(flops=2**29, bytes_accessed=2**21, transcendentals=2048),
    )(queries, keys, values, carried)


def project_kernel(n_ref, w_ref, o_ref):
    n = n_ref[...]
    w = jnp.concatenate([w_ref[0, c, x] for x in range(X) for c in range(C)], axis=0)
    o = lax.dot_general(n, w, (((1,), (1,)), ((), ())), preferred_element_type=F32)
    o_ref[...] = o.astype(BF16)


def project(normed, weight):
    return pl.pallas_call(
        project_kernel,
        grid=(Z,),
        in_specs=[
            pl.BlockSpec((512, 512), lambda z: (0, 0)),
            pl.BlockSpec((1, C, X, 64, 512), lambda z: (z, 0, 0, 0, 0)),
        ],
        out_specs=pl.BlockSpec((512, 512), lambda z: (0, z)),
        out_shape=jax.ShapeDtypeStruct((512, 4096), BF16),
        compiler_params=pltpu.CompilerParams(vmem_limit_bytes=24 * 2**20),
        cost_estimate=pl.CostEstimate(flops=2**31, bytes_accessed=2**23, transcendentals=0),
    )(normed, weight)


def everywhere(part, axis, size):
    return lax.all_to_all(jnp.broadcast_to(part[None], (size,) + part.shape), axis, 0, 0)


def on_device(queries, keys, values, out_weight):
    plane = ("x", "core")
    w_x = everywhere(out_weight.T, "x", X)
    w_x, keys, values = lax.optimization_barrier((w_x, keys, values))
    weight = lax.all_gather(w_x.reshape(X * 64, 512), ("z", "core"), axis=0, tiled=True)
    weight = weight.reshape(Z, C, X, 64, 512)

    state = states(keys, values).reshape(8, 64, HD)
    pieces = lax.all_to_all(state, plane, 0, 0).astype(F32)
    place = lax.axis_index("z")
    running = jnp.zeros((64, HD), F32)
    earlier = []
    for i in range(8):
        earlier.append(running)
        running = running + pieces[i]
    earlier = jnp.stack(earlier)
    totals = everywhere(running.astype(BF16), "z", Z)
    mask = (jnp.arange(Z) < place)[:, None, None]
    before = jnp.sum(jnp.where(mask, totals, 0).astype(F32), axis=0)
    carried = (earlier + before[None]).astype(BF16)
    carried = lax.all_to_all(carried, plane, 0, 0).reshape(4 * HD, HD)

    normed = attention(queries, keys, values, carried)
    terms = project(normed, weight)
    return lax.psum_scatter(terms, "tp", scatter_dimension=0, tiled=True)


def solution(mesh):
    split = Mesh(mesh.devices.reshape(Z, X, C, Y), ("z", "x", "core", "tp"))
    ctx = ("z", "x", "core")
    placed = (P(ctx, "tp"), P(ctx, "tp"), P(ctx, "tp"), P("tp", ctx))
    return jax.shard_map(
        on_device, mesh=split, in_specs=placed, out_specs=P((*ctx, "tp"), None), check_vma=False
    )
```

```python
import jax
import jax.numpy as jnp
from jax import lax
from jax.experimental import pallas as pl
from jax.experimental.pallas import tpu as pltpu
from jax.sharding import Mesh, PartitionSpec as P

HD = 128
F32 = jnp.float32
BF16 = jnp.bfloat16
Z, X, C, Y = 8, 4, 2, 8
MIB = 2**20
NT = (((1,), (1,)), ((), ()))
TN = (((0,), (0,)), ((), ()))
VMEM = pl.BlockSpec(memory_space=pltpu.VMEM)
SMEM = pl.BlockSpec(memory_space=pltpu.SMEM)


def call(kernel, out_shape, operands, flops, moved, scalars=0, vmem=24):
    return pl.pallas_call(
        kernel,
        out_shape=out_shape,
        in_specs=[SMEM] * scalars + [VMEM] * (len(operands) - scalars),
        out_specs=jax.tree.map(lambda _: VMEM, out_shape),
        compiler_params=pltpu.CompilerParams(vmem_limit_bytes=vmem * MIB),
        cost_estimate=pl.CostEstimate(flops=flops, bytes_accessed=moved, transcendentals=0),
    )(*operands)


def state_kernel(k_ref, v_ref, s_ref):
    for h in range(4):
        cols = slice(h * HD, (h + 1) * HD)
        s = lax.dot_general(k_ref[:, cols], v_ref[:, cols], TN, preferred_element_type=F32)
        s_ref[cols, :] = s.astype(BF16)


def plane_kernel(p_ref, e_ref, t_ref):
    running = jnp.zeros(p_ref.shape[1:], F32)
    for i in range(C * X):
        e_ref[i] = running
        running = running + p_ref[i].astype(F32)
    total = running.astype(BF16)
    for i in range(Z):
        t_ref[i] = total


def carry_kernel(z_ref, t_ref, e_ref, c_ref):
    z = z_ref[0]
    before = jnp.zeros(t_ref.shape[1:], F32)
    for i in range(Z - 1):
        before = before + jnp.where(i < z, t_ref[i].astype(F32), 0.0)
    for i in range(C * X):
        c_ref[i] = (e_ref[i] + before).astype(BF16)


def attention_kernel(q_ref, k_ref, v_ref, c_ref, o_ref):
    half = 256
    row = lax.broadcasted_iota(jnp.int32, (half, half), 0)
    col = lax.broadcasted_iota(jnp.int32, (half, half), 1)
    causal = row >= col

    def masked(q, k):
        s = lax.dot_general(q, k, NT, preferred_element_type=F32)
        return jnp.where(causal, s, 0.0).astype(BF16)

    def norm(a):
        r = lax.rsqrt(jnp.mean(a * a, axis=-1, keepdims=True) + 1e-06)
        return (a * r).astype(BF16)

    for h in range(4):
        cols = slice(h * HD, (h + 1) * HD)
        c = c_ref[cols]
        q0, q1 = q_ref[:half, cols], q_ref[half:, cols]
        k0, k1 = k_ref[:half, cols], k_ref[half:, cols]
        v0, v1 = v_ref[:half, cols], v_ref[half:, cols]
        a0 = jnp.dot(q0, c, preferred_element_type=F32)
        a0 += jnp.dot(masked(q0, k0), v0, preferred_element_type=F32)
        o_ref[:half, cols] = norm(a0)
        a1 = jnp.dot(q1, c, preferred_element_type=F32)
        s10 = lax.dot_general(q1, k0, NT, preferred_element_type=F32).astype(BF16)
        a1 += jnp.dot(s10, v0, preferred_element_type=F32)
        a1 += jnp.dot(masked(q1, k1), v1, preferred_element_type=F32)
        o_ref[half:, cols] = norm(a1)


SHIFTS = (4, 3, 5, 2, 6, 1, 7, 0)


def project_kernel(y_ref, n_ref, w_ref, up_ref, down_ref, *refs):
    rest_refs, rows = refs[:-1], refs[-1]
    z = pl.program_id(0)

    @pl.when(z == 0)
    def _():
        for i, shift in enumerate(SHIFTS):
            at = pl.multiple_of(lax.rem(y_ref[0] + shift, Y) * 64, 64)
            rows[i * 64 : (i + 1) * 64] = n_ref[pl.ds(at, 64)]

    w = jnp.concatenate([w_ref[0, c, x] for x in range(X) for c in range(C)], axis=0)
    o = lax.dot_general(rows[...], w, NT, preferred_element_type=F32).astype(BF16)

    @pl.when(z < Z // 2)
    def _():
        up_ref[...] = o[:64]

    @pl.when(z >= Z // 2)
    def _():
        down_ref[...] = o[:64]

    for i, ref in enumerate(rest_refs):
        ref[...] = o[(i + 1) * 64 : (i + 2) * 64]


def project(y, normed, weight):
    half = Z // 2
    out = pl.BlockSpec((64, 512), lambda z: (0, z))
    up = pl.BlockSpec((64, 512), lambda z: (0, jnp.minimum(z, half - 1)))
    down = pl.BlockSpec((64, 512), lambda z: (0, jnp.maximum(z - half, 0)))
    return pl.pallas_call(
        project_kernel,
        grid=(Z,),
        in_specs=[
            SMEM,
            pl.BlockSpec((512, 512), lambda z: (0, 0)),
            pl.BlockSpec((1, C, X, 64, 512), lambda z: (z, 0, 0, 0, 0)),
        ],
        out_specs=[up, down] + [out] * 7,
        out_shape=[shape(64, 2048)] * 2 + [shape(64, 4096)] * 7,
        scratch_shapes=[pltpu.VMEM((512, 512), BF16)],
        compiler_params=pltpu.CompilerParams(vmem_limit_bytes=56 * MIB),
        cost_estimate=pl.CostEstimate(flops=2**31, bytes_accessed=8 * MIB, transcendentals=0),
    )(y, normed, weight)


def everywhere(part, axis, size):
    return lax.all_to_all(jnp.broadcast_to(part[None], (size,) + part.shape), axis, 0, 0)


def shape(*dims, dtype=BF16):
    return jax.ShapeDtypeStruct(dims, dtype)


def add(a, b):
    return (a.astype(F32) + b.astype(F32)).astype(BF16)


def on_device(queries, keys, values, out_weight):
    plane = ("x", "core")
    z, y = (lax.axis_index(a).astype(jnp.int32)[None] for a in ("z", "tp"))

    w_x = everywhere(out_weight.T, "x", X)
    state = call(state_kernel, shape(4 * HD, HD), (keys, values), 2**26, MIB, vmem=16)
    state, w_x = lax.optimization_barrier((state, w_x))
    weight = lax.all_gather(w_x.reshape(X * 64, 512), ("z", "core"), axis=0, tiled=True)
    weight = weight.reshape(Z, C, X, 64, 512)
    pieces = lax.all_to_all(state.reshape(8, 64, HD), plane, 0, 0)
    earlier, total = call(
        plane_kernel, (shape(8, 64, HD, dtype=F32), shape(8, 64, HD)), (pieces,), 2**17, 2**19, vmem=8
    )
    totals = lax.all_to_all(total, "z", 0, 0)
    carried = call(carry_kernel, shape(8, 64, HD), (z, totals, earlier), 2**18, 2**19, 1, vmem=8)
    carried = lax.all_to_all(carried, plane, 0, 0).reshape(4 * HD, HD)
    normed = call(
        attention_kernel, shape(512, 512), (queries, keys, values, carried), 2**29, 2 * MIB
    )

    up, down, u3, d3, u2, d2, u1, d1, mine = project(y, normed, weight)
    ring_up = [(i, (i + 1) % Y) for i in range(Y)]
    ring_down = [(i, (i - 1) % Y) for i in range(Y)]
    up = lax.ppermute(up, "tp", ring_up)
    down = lax.ppermute(down, "tp", ring_down)
    up = add(u3, jnp.pad(up, ((0, 0), (0, 2048))))
    down = add(d3, jnp.pad(down, ((0, 0), (2048, 0))))
    up = lax.ppermute(up, "tp", ring_up)
    down = lax.ppermute(down, "tp", ring_down)
    for u, d in ((u2, d2), (u1, d1)):
        up = lax.ppermute(add(u, up), "tp", ring_up)
        down = lax.ppermute(add(d, down), "tp", ring_down)
    return (mine.astype(F32) + up.astype(F32) + down.astype(F32)).astype(BF16)


def solution(mesh):
    split = Mesh(mesh.devices.reshape(Z, X, C, Y), ("z", "x", "core", "tp"))
    ctx = ("z", "x", "core")
    placed = (P(ctx, "tp"), P(ctx, "tp"), P(ctx, "tp"), P("tp", ctx))
    return jax.shard_map(
        on_device, mesh=split, in_specs=placed, out_specs=P((*ctx, "tp"), None), check_vma=False
    )
```

```python
import jax
import jax.numpy as jnp
from jax import lax
from jax.experimental import pallas as pl
from jax.experimental.pallas import tpu as pltpu
from jax.sharding import Mesh, PartitionSpec as P

HD = 128
F32 = jnp.float32
BF16 = jnp.bfloat16
Z, X, C, Y = 8, 4, 2, 8
MIB = 2**20
NT = (((1,), (1,)), ((), ()))
TN = (((0,), (0,)), ((), ()))
VMEM = pl.BlockSpec(memory_space=pltpu.VMEM)
SMEM = pl.BlockSpec(memory_space=pltpu.SMEM)


def call(kernel, out_shape, operands, flops, moved, scalars=0, vmem=24):
    return pl.pallas_call(
        kernel,
        out_shape=out_shape,
        in_specs=[SMEM] * scalars + [VMEM] * (len(operands) - scalars),
        out_specs=jax.tree.map(lambda _: VMEM, out_shape),
        compiler_params=pltpu.CompilerParams(vmem_limit_bytes=vmem * MIB),
        cost_estimate=pl.CostEstimate(flops=flops, bytes_accessed=moved, transcendentals=0),
    )(*operands)


def state_kernel(k_ref, v_ref, s_ref):
    for h in range(4):
        cols = slice(h * HD, (h + 1) * HD)
        s = lax.dot_general(k_ref[:, cols], v_ref[:, cols], TN, preferred_element_type=F32)
        s_ref[cols, :] = s.astype(BF16)


def plane_kernel(p_ref, e_ref, t_ref):
    running = jnp.zeros(p_ref.shape[1:], F32)
    for i in range(C * X):
        e_ref[i] = running
        running = running + p_ref[i].astype(F32)
    total = running.astype(BF16)
    for i in range(Z):
        t_ref[i] = total


def carry_kernel(z_ref, t_ref, e_ref, c_ref):
    z = z_ref[0]
    before = jnp.zeros(t_ref.shape[1:], F32)
    for i in range(Z - 1):
        before = before + jnp.where(i < z, t_ref[i].astype(F32), 0.0)
    for i in range(C * X):
        c_ref[i] = (e_ref[i] + before).astype(BF16)


def attention_kernel(q_ref, k_ref, v_ref, c_ref, o_ref):
    half = 256
    row = lax.broadcasted_iota(jnp.int32, (half, half), 0)
    col = lax.broadcasted_iota(jnp.int32, (half, half), 1)
    causal = row >= col

    def masked(q, k):
        s = lax.dot_general(q, k, NT, preferred_element_type=F32)
        return jnp.where(causal, s, 0.0).astype(BF16)

    def norm(a):
        r = lax.rsqrt(jnp.mean(a * a, axis=-1, keepdims=True) + 1e-06)
        return (a * r).astype(BF16)

    for h in range(4):
        cols = slice(h * HD, (h + 1) * HD)
        c = c_ref[cols]
        q0, q1 = q_ref[:half, cols], q_ref[half:, cols]
        k0, k1 = k_ref[:half, cols], k_ref[half:, cols]
        v0, v1 = v_ref[:half, cols], v_ref[half:, cols]
        a0 = jnp.dot(q0, c, preferred_element_type=F32)
        a0 += jnp.dot(masked(q0, k0), v0, preferred_element_type=F32)
        o_ref[:half, cols] = norm(a0)
        a1 = jnp.dot(q1, c, preferred_element_type=F32)
        s10 = lax.dot_general(q1, k0, NT, preferred_element_type=F32).astype(BF16)
        a1 += jnp.dot(s10, v0, preferred_element_type=F32)
        a1 += jnp.dot(masked(q1, k1), v1, preferred_element_type=F32)
        o_ref[half:, cols] = norm(a1)


def project(n_ref, y, shifts, own_ref, other_ref, store):
    rows = [n_ref[pl.ds(pl.multiple_of(lax.rem(y + s, Y) * 64, 64), 64), :] for s in shifts]
    n = jnp.concatenate(rows, axis=0)
    for t in range(8):
        parts = []
        for i in range(4):
            x, z = divmod(4 * t + i, Z)
            parts += [own_ref[x, z], other_ref[x, z]]
        o = lax.dot_general(n, jnp.concatenate(parts, axis=0), NT, preferred_element_type=F32)
        store(t, o.astype(BF16))


def first_kernel(y_ref, n_ref, own_ref, other_ref, up_ref, down_ref):
    def store(t, o):
        ref = up_ref if t < 4 else down_ref
        ref[:, t % 4 * 512 : t % 4 * 512 + 512] = o

    project(n_ref, y_ref[0], (4,), own_ref, other_ref, store)


def rest_kernel(y_ref, n_ref, own_ref, other_ref, *out_refs):
    def store(t, o):
        for i, ref in enumerate(out_refs):
            ref[:, t * 512 : (t + 1) * 512] = o[i * 64 : (i + 1) * 64]

    project(n_ref, y_ref[0], (3, 5, 2, 6, 1, 7, 0), own_ref, other_ref, store)


def half_step_kernel(u_ref, up_ref, d_ref, down_ref, uo_ref, do_ref):
    uo_ref[:, :2048] = add(u_ref[:, :2048], up_ref[...])
    uo_ref[:, 2048:] = u_ref[:, 2048:]
    do_ref[:, :2048] = d_ref[:, :2048]
    do_ref[:, 2048:] = add(d_ref[:, 2048:], down_ref[...])


def step_kernel(u_ref, up_ref, d_ref, down_ref, uo_ref, do_ref):
    uo_ref[...] = add(u_ref[...], up_ref[...])
    do_ref[...] = add(d_ref[...], down_ref[...])


def last_kernel(place_ref, m_ref, up_ref, down_ref, o_ref):
    x, core = place_ref[0], place_ref[1]
    for t in range(X * Z):
        dx, z = divmod(t, Z)
        cols = slice(t * 128, (t + 1) * 128)
        o = m_ref[:, cols].astype(F32) + up_ref[:, cols].astype(F32) + down_ref[:, cols].astype(F32)
        o = jnp.where(core == 0, o, pltpu.roll(o, 64, 1))
        at = pl.multiple_of((z * X + lax.rem(x + dx, X)) * 128, 128)
        o_ref[:, pl.ds(at, 128)] = o.astype(BF16)


def everywhere(part, axis, size):
    return lax.all_to_all(jnp.broadcast_to(part[None], (size,) + part.shape), axis, 0, 0)


def shape(*dims, dtype=BF16):
    return jax.ShapeDtypeStruct(dims, dtype)


def add(a, b):
    return (a.astype(F32) + b.astype(F32)).astype(BF16)


def on_device(queries, keys, values, out_weight):
    plane = ("x", "core")
    z, x, y, core = (lax.axis_index(a).astype(jnp.int32) for a in ("z", "x", "tp", "core"))

    w_z = everywhere(out_weight.T, "z", Z)
    state = call(state_kernel, shape(4 * HD, HD), (keys, values), 2**26, MIB, vmem=16)
    state, w_z = lax.optimization_barrier((state, w_z))
    pieces = lax.all_to_all(state.reshape(8, 64, HD), plane, 0, 0)
    pieces, w_z = lax.optimization_barrier((pieces, w_z))
    own = [w_z] + [lax.ppermute(w_z, "x", [((i + d) % X, i) for i in range(X)]) for d in (1, 2, 3)]
    earlier, total = call(
        plane_kernel, (shape(8, 64, HD, dtype=F32), shape(8, 64, HD)), (pieces,), 2**17, 2**19, vmem=8
    )
    totals = lax.all_to_all(total, "z", 0, 0)
    carried = call(carry_kernel, shape(8, 64, HD), (z[None], totals, earlier), 2**18, 2**19, 1, vmem=8)
    carried = lax.all_to_all(carried, plane, 0, 0).reshape(4 * HD, HD)
    carried, *own = lax.optimization_barrier((carried, *own))
    own = jnp.stack(own)
    other = lax.ppermute(own, "core", [(0, 1), (1, 0)])
    normed = call(
        attention_kernel, shape(512, 512), (queries, keys, values, carried), 2**29, 2 * MIB
    )

    operands = (y[None], normed, own, other)
    up, down = call(first_kernel, (shape(64, 2048),) * 2, operands, 2**28, 5 * MIB, 1)
    u3, d3, u2, d2, u1, d1, mine = call(
        rest_kernel, (shape(64, 4096),) * 7, operands, 2**31, 8 * MIB, 1, vmem=32
    )

    def ring(up, down):
        up = lax.ppermute(up, "tp", [(i, (i + 1) % Y) for i in range(Y)])
        down = lax.ppermute(down, "tp", [(i, (i - 1) % Y) for i in range(Y)])
        return lax.optimization_barrier((up, down))

    up, down = ring(up, down)
    for kernel, u, d in ((half_step_kernel, u3, d3), (step_kernel, u2, d2), (step_kernel, u1, d1)):
        up, down = call(kernel, (shape(64, 4096),) * 2, (u, up, d, down), 2**20, 3 * MIB, vmem=16)
        up, down = ring(up, down)
    place = jnp.stack([x, core])
    return call(last_kernel, shape(64, 4096), (place, mine, up, down), 2**20, 2 * MIB, 1, vmem=16)


def solution(mesh):
    split = Mesh(mesh.devices.reshape(Z, X, C, Y), ("z", "x", "core", "tp"))
    ctx = ("z", "x", "core")
    placed = (P(ctx, "tp"), P(ctx, "tp"), P(ctx, "tp"), P("tp", ctx))
    return jax.shard_map(
        on_device, mesh=split, in_specs=placed, out_specs=P((*ctx, "tp"), None), check_vma=False
    )
```

```python
import jax
import jax.numpy as jnp
from jax import lax
from jax.experimental import pallas as pl
from jax.experimental.pallas import tpu as pltpu
from jax.sharding import Mesh, PartitionSpec as P

HD = 128
F32 = jnp.float32
BF16 = jnp.bfloat16
Z, X, C, Y = 8, 4, 2, 8
MIB = 2**20
NT = (((1,), (1,)), ((), ()))
TN = (((0,), (0,)), ((), ()))
VMEM = pl.BlockSpec(memory_space=pltpu.VMEM)
SMEM = pl.BlockSpec(memory_space=pltpu.SMEM)


def call(kernel, out_shape, operands, flops, moved, scalars=0, vmem=24):
    return pl.pallas_call(
        kernel,
        out_shape=out_shape,
        in_specs=[SMEM] * scalars + [VMEM] * (len(operands) - scalars),
        out_specs=jax.tree.map(lambda _: VMEM, out_shape),
        compiler_params=pltpu.CompilerParams(vmem_limit_bytes=vmem * MIB),
        cost_estimate=pl.CostEstimate(flops=flops, bytes_accessed=moved, transcendentals=0),
    )(*operands)


def plane_kernel(p_ref, e_ref, t_ref):
    running = jnp.zeros(p_ref.shape[1:], F32)
    for i in range(C * X):
        e_ref[i] = running
        running = running + p_ref[i].astype(F32)
    total = running.astype(BF16)
    for i in range(Z):
        t_ref[i] = total


def carry_kernel(z_ref, t_ref, e_ref, c_ref):
    z = z_ref[0]
    before = jnp.zeros(t_ref.shape[1:], F32)
    for i in range(Z - 1):
        before = before + jnp.where(i < z, t_ref[i].astype(F32), 0.0)
    for i in range(C * X):
        c_ref[i] = (e_ref[i] + before).astype(BF16)


def state_kernel(k_ref, v_ref, s_ref):
    s = lax.dot_general(k_ref[...], v_ref[...], TN, preferred_element_type=F32)
    s_ref[...] = s.astype(BF16)


def states(keys, values):
    by_head = pl.BlockSpec((512, HD), lambda h: (0, h))
    return pl.pallas_call(
        state_kernel,
        grid=(4,),
        in_specs=[by_head, by_head],
        out_specs=pl.BlockSpec((HD, HD), lambda h: (h, 0)),
        out_shape=shape(4 * HD, HD),
        compiler_params=pltpu.CompilerParams(vmem_limit_bytes=56 * MIB),
        cost_estimate=pl.CostEstimate(flops=2**26, bytes_accessed=MIB, transcendentals=0),
    )(keys, values)


def attention_kernel(q_ref, k_ref, v_ref, c_ref, o_ref):
    half = 256
    row = lax.broadcasted_iota(jnp.int32, (half, half), 0)
    col = lax.broadcasted_iota(jnp.int32, (half, half), 1)
    causal = row >= col
    nt = (((1,), (1,)), ((), ()))

    def masked(q, k):
        s = lax.dot_general(q, k, nt, preferred_element_type=F32)
        return jnp.where(causal, s, 0.0).astype(BF16)

    def norm(a):
        r = lax.rsqrt(jnp.mean(a * a, axis=-1, keepdims=True) + 1e-06)
        return (a * r).astype(BF16)

    c = c_ref[...]
    q0, q1 = q_ref[:half], q_ref[half:]
    k0, k1 = k_ref[:half], k_ref[half:]
    v0, v1 = v_ref[:half], v_ref[half:]
    a0 = jnp.dot(q0, c, preferred_element_type=F32)
    a0 += jnp.dot(masked(q0, k0), v0, preferred_element_type=F32)
    o_ref[:half] = norm(a0)
    a1 = jnp.dot(q1, c, preferred_element_type=F32)
    s10 = lax.dot_general(q1, k0, nt, preferred_element_type=F32).astype(BF16)
    a1 += jnp.dot(s10, v0, preferred_element_type=F32)
    a1 += jnp.dot(masked(q1, k1), v1, preferred_element_type=F32)
    o_ref[half:] = norm(a1)


def attention(queries, keys, values, carried):
    by_head = pl.BlockSpec((512, HD), lambda h: (0, h))
    return pl.pallas_call(
        attention_kernel,
        grid=(4,),
        in_specs=[by_head, by_head, by_head, pl.BlockSpec((HD, HD), lambda h: (h, 0))],
        out_specs=by_head,
        out_shape=jax.ShapeDtypeStruct((512, 512), BF16),
        compiler_params=pltpu.CompilerParams(vmem_limit_bytes=56 * MIB),
        cost_estimate=pl.CostEstimate(flops=2**29, bytes_accessed=2**21, transcendentals=2048),
    )(queries, keys, values, carried)


def project_kernel(n_ref, w_ref, o_ref):
    n = n_ref[...]
    w = jnp.concatenate([w_ref[0, c, x] for x in range(X) for c in range(C)], axis=0)
    o = lax.dot_general(n, w, (((1,), (1,)), ((), ())), preferred_element_type=F32)
    o_ref[...] = o.astype(BF16)


def project(normed, weight):
    return pl.pallas_call(
        project_kernel,
        grid=(Z,),
        in_specs=[
            pl.BlockSpec((512, 512), lambda z: (0, 0)),
            pl.BlockSpec((1, C, X, 64, 512), lambda z: (z, 0, 0, 0, 0)),
        ],
        out_specs=pl.BlockSpec((512, 512), lambda z: (0, z)),
        out_shape=jax.ShapeDtypeStruct((512, 4096), BF16),
        compiler_params=pltpu.CompilerParams(vmem_limit_bytes=56 * MIB),
        cost_estimate=pl.CostEstimate(flops=2**31, bytes_accessed=2**23, transcendentals=0),
    )(normed, weight)


def shape(*dims, dtype=BF16):
    return jax.ShapeDtypeStruct(dims, dtype)


def everywhere(part, axis, size):
    return lax.all_to_all(jnp.broadcast_to(part[None], (size,) + part.shape), axis, 0, 0)


def on_device(queries, keys, values, out_weight):
    plane = ("x", "core")
    w_x = everywhere(out_weight.T, "x", X)
    w_x, keys, values = lax.optimization_barrier((w_x, keys, values))
    weight = lax.all_gather(w_x.reshape(X * 64, 512), ("z", "core"), axis=0, tiled=True)
    weight = weight.reshape(Z, C, X, 64, 512)

    state = states(keys, values).reshape(8, 64, HD)
    pieces = lax.all_to_all(state, plane, 0, 0)
    earlier, total = call(
        plane_kernel, (shape(8, 64, HD, dtype=F32), shape(8, 64, HD)), (pieces,), 2**17, 2**19, vmem=8
    )
    totals = lax.all_to_all(total, "z", 0, 0)
    z = lax.axis_index("z").astype(jnp.int32)[None]
    carried = call(carry_kernel, shape(8, 64, HD), (z, totals, earlier), 2**18, 2**19, 1, vmem=8)
    carried = lax.all_to_all(carried, plane, 0, 0).reshape(4 * HD, HD)

    normed = attention(queries, keys, values, carried)
    terms = project(normed, weight)
    return lax.psum_scatter(terms, "tp", scatter_dimension=0, tiled=True)


def solution(mesh):
    split = Mesh(mesh.devices.reshape(Z, X, C, Y), ("z", "x", "core", "tp"))
    ctx = ("z", "x", "core")
    placed = (P(ctx, "tp"), P(ctx, "tp"), P(ctx, "tp"), P("tp", ctx))
    return jax.shard_map(
        on_device, mesh=split, in_specs=placed, out_specs=P((*ctx, "tp"), None), check_vma=False
    )
```

```python
import jax
import jax.numpy as jnp
from jax import lax
from jax.experimental import pallas as pl
from jax.experimental.pallas import tpu as pltpu
from jax.sharding import Mesh, PartitionSpec as P

HD = 128
F32 = jnp.float32
BF16 = jnp.bfloat16
Z, X, C, Y = 8, 4, 2, 8
MIB = 2**20
NT = (((1,), (1,)), ((), ()))
TN = (((0,), (0,)), ((), ()))
VMEM = pl.BlockSpec(memory_space=pltpu.VMEM)
SMEM = pl.BlockSpec(memory_space=pltpu.SMEM)
HBM = pl.BlockSpec(memory_space=pltpu.HBM)


def call(kernel, out_shape, operands, flops, moved, scalars=0, vmem=24):
    return pl.pallas_call(
        kernel,
        out_shape=out_shape,
        in_specs=[SMEM] * scalars + [VMEM] * (len(operands) - scalars),
        out_specs=jax.tree.map(lambda _: VMEM, out_shape),
        compiler_params=pltpu.CompilerParams(vmem_limit_bytes=vmem * MIB),
        cost_estimate=pl.CostEstimate(flops=flops, bytes_accessed=moved, transcendentals=0),
    )(*operands)


def plane_kernel(p_ref, e_ref, t_ref):
    running = jnp.zeros(p_ref.shape[1:], F32)
    for i in range(C * X):
        e_ref[i] = running
        running = running + p_ref[i].astype(F32)
    total = running.astype(BF16)
    for i in range(Z):
        t_ref[i] = total


def carry_kernel(z_ref, t_ref, e_ref, c_ref):
    z = z_ref[0]
    before = jnp.zeros(t_ref.shape[1:], F32)
    for i in range(Z - 1):
        before = before + jnp.where(i < z, t_ref[i].astype(F32), 0.0)
    for i in range(C * X):
        c_ref[i] = (e_ref[i] + before).astype(BF16)


def fetch(sources, buffers, sems):
    copies = [
        pltpu.make_async_copy(source, buffer, sems.at[i])
        for i, (source, buffer) in enumerate(zip(sources, buffers))
    ]
    for copy in copies:
        copy.start()
    for copy in copies:
        copy.wait()


def state_kernel(k_hbm, v_hbm, s_ref, k_ref, v_ref, sems):
    fetch((k_hbm, v_hbm), (k_ref, v_ref), sems)
    for h in range(4):
        cols = slice(h * HD, (h + 1) * HD)
        s = lax.dot_general(k_ref[:, cols], v_ref[:, cols], TN, preferred_element_type=F32)
        s_ref[cols, :] = s.astype(BF16)


def states(keys, values):
    return pl.pallas_call(
        state_kernel,
        in_specs=[HBM] * 2,
        out_specs=VMEM,
        out_shape=shape(4 * HD, HD),
        scratch_shapes=[pltpu.VMEM((512, 512), BF16)] * 2 + [pltpu.SemaphoreType.DMA((2,))],
        compiler_params=pltpu.CompilerParams(vmem_limit_bytes=56 * MIB),
        cost_estimate=pl.CostEstimate(flops=2**26, bytes_accessed=MIB, transcendentals=0),
    )(keys, values)


def attention_kernel(q_hbm, k_hbm, v_hbm, c_ref, o_ref, q_ref, k_ref, v_ref, sems):
    fetch((q_hbm, k_hbm, v_hbm), (q_ref, k_ref, v_ref), sems)
    half = 256
    row = lax.broadcasted_iota(jnp.int32, (half, half), 0)
    col = lax.broadcasted_iota(jnp.int32, (half, half), 1)
    causal = row >= col

    def masked(q, k):
        s = lax.dot_general(q, k, NT, preferred_element_type=F32)
        return jnp.where(causal, s, 0.0).astype(BF16)

    def norm(a):
        r = lax.rsqrt(jnp.mean(a * a, axis=-1, keepdims=True) + 1e-06)
        return (a * r).astype(BF16)

    for h in range(4):
        cols = slice(h * HD, (h + 1) * HD)
        c = c_ref[cols]
        q0, q1 = q_ref[:half, cols], q_ref[half:, cols]
        k0, k1 = k_ref[:half, cols], k_ref[half:, cols]
        v0, v1 = v_ref[:half, cols], v_ref[half:, cols]
        a0 = jnp.dot(q0, c, preferred_element_type=F32)
        a0 += jnp.dot(masked(q0, k0), v0, preferred_element_type=F32)
        o_ref[:half, cols] = norm(a0)
        a1 = jnp.dot(q1, c, preferred_element_type=F32)
        s10 = lax.dot_general(q1, k0, NT, preferred_element_type=F32).astype(BF16)
        a1 += jnp.dot(s10, v0, preferred_element_type=F32)
        a1 += jnp.dot(masked(q1, k1), v1, preferred_element_type=F32)
        o_ref[half:, cols] = norm(a1)


def attention(queries, keys, values, carried):
    return pl.pallas_call(
        attention_kernel,
        in_specs=[HBM] * 3 + [VMEM],
        out_specs=VMEM,
        out_shape=shape(512, 512),
        scratch_shapes=[pltpu.VMEM((512, 512), BF16)] * 3 + [pltpu.SemaphoreType.DMA((3,))],
        compiler_params=pltpu.CompilerParams(vmem_limit_bytes=56 * MIB),
        cost_estimate=pl.CostEstimate(flops=2**29, bytes_accessed=2 * MIB, transcendentals=2048),
    )(queries, keys, values, carried)


def project_kernel(n_ref, w_hbm, o_hbm, w_buf, o_buf, in_sems, out_sems):
    incoming = [pltpu.make_async_copy(w_hbm.at[z], w_buf.at[z], in_sems.at[z]) for z in range(Z)]
    for copy in incoming:
        copy.start()
    n = n_ref[...]
    outgoing = []
    for z in range(Z):
        incoming[z].wait()
        w = jnp.concatenate([w_buf[z, c, x] for x in range(X) for c in range(C)], axis=0)
        o = lax.dot_general(n, w, NT, preferred_element_type=F32)
        cols = slice(z * 512, (z + 1) * 512)
        o_buf[:, cols] = o.astype(BF16)
        copy = pltpu.make_async_copy(o_buf.at[:, cols], o_hbm.at[:, cols], out_sems.at[z])
        copy.start()
        outgoing.append(copy)
    for copy in outgoing:
        copy.wait()


def project(normed, weight):
    return pl.pallas_call(
        project_kernel,
        in_specs=[VMEM, HBM],
        out_specs=HBM,
        out_shape=shape(512, 4096),
        scratch_shapes=[
            pltpu.VMEM((Z, C, X, 64, 512), BF16),
            pltpu.VMEM((512, 4096), BF16),
            pltpu.SemaphoreType.DMA((Z,)),
            pltpu.SemaphoreType.DMA((Z,)),
        ],
        compiler_params=pltpu.CompilerParams(vmem_limit_bytes=56 * MIB),
        cost_estimate=pl.CostEstimate(flops=2**31, bytes_accessed=8 * MIB, transcendentals=0),
    )(normed, weight)


def shape(*dims, dtype=BF16):
    return jax.ShapeDtypeStruct(dims, dtype)


def everywhere(part, axis, size):
    return lax.all_to_all(jnp.broadcast_to(part[None], (size,) + part.shape), axis, 0, 0)


def on_device(queries, keys, values, out_weight):
    plane = ("x", "core")
    w_x = everywhere(out_weight.T, "x", X)
    w_x, keys = lax.optimization_barrier((w_x, keys))
    weight = lax.all_gather(w_x.reshape(X * 64, 512), ("z", "core"), axis=0, tiled=True)
    weight = weight.reshape(Z, C, X, 64, 512)

    state = states(keys, values).reshape(8, 64, HD)
    pieces = lax.all_to_all(state, plane, 0, 0)
    earlier, total = call(
        plane_kernel, (shape(8, 64, HD, dtype=F32), shape(8, 64, HD)), (pieces,), 2**17, 2**19, vmem=8
    )
    totals = lax.all_to_all(total, "z", 0, 0)
    z = lax.axis_index("z").astype(jnp.int32)[None]
    carried = call(carry_kernel, shape(8, 64, HD), (z, totals, earlier), 2**18, 2**19, 1, vmem=8)
    carried = lax.all_to_all(carried, plane, 0, 0).reshape(4 * HD, HD)

    normed = attention(queries, keys, values, carried)
    terms = project(normed, weight)
    return lax.psum_scatter(terms, "tp", scatter_dimension=0, tiled=True)


def solution(mesh):
    split = Mesh(mesh.devices.reshape(Z, X, C, Y), ("z", "x", "core", "tp"))
    ctx = ("z", "x", "core")
    placed = (P(ctx, "tp"), P(ctx, "tp"), P(ctx, "tp"), P("tp", ctx))
    return jax.shard_map(
        on_device, mesh=split, in_specs=placed, out_specs=P((*ctx, "tp"), None), check_vma=False
    )
```

```python
import jax
import jax.numpy as jnp
from jax import lax
from jax.experimental import pallas as pl
from jax.experimental.pallas import tpu as pltpu
from jax.sharding import Mesh, PartitionSpec as P

HD = 128
F32 = jnp.float32
BF16 = jnp.bfloat16
Z, X, C, Y = 8, 4, 2, 8
MAIN, SIDE = 6, 2
SHIFTS = (4, 3, 5, 2, 6, 1, 7, 0)
MIB = 2**20
NT = (((1,), (1,)), ((), ()))
TN = (((0,), (0,)), ((), ()))
VMEM = pl.BlockSpec(memory_space=pltpu.VMEM)
SMEM = pl.BlockSpec(memory_space=pltpu.SMEM)
HBM = pl.BlockSpec(memory_space=pltpu.HBM)


def call(kernel, out_shape, operands, flops, moved, scalars=0, vmem=24):
    return pl.pallas_call(
        kernel,
        out_shape=out_shape,
        in_specs=[SMEM] * scalars + [VMEM] * (len(operands) - scalars),
        out_specs=jax.tree.map(lambda _: VMEM, out_shape),
        compiler_params=pltpu.CompilerParams(vmem_limit_bytes=vmem * MIB),
        cost_estimate=pl.CostEstimate(flops=flops, bytes_accessed=moved, transcendentals=0),
    )(*operands)


def plane_kernel(p_ref, e_ref, t_ref):
    running = jnp.zeros(p_ref.shape[1:], F32)
    for i in range(C * X):
        e_ref[i] = running
        running = running + p_ref[i].astype(F32)
    total = running.astype(BF16)
    for i in range(Z):
        t_ref[i] = total


def carry_kernel(z_ref, t_ref, e_ref, c_ref):
    z = z_ref[0]
    before = jnp.zeros(t_ref.shape[1:], F32)
    for i in range(Z - 1):
        before = before + jnp.where(i < z, t_ref[i].astype(F32), 0.0)
    for i in range(C * X):
        c_ref[i] = (e_ref[i] + before).astype(BF16)


def fetch(sources, buffers, sems):
    copies = [
        pltpu.make_async_copy(source, buffer, sems.at[i])
        for i, (source, buffer) in enumerate(zip(sources, buffers))
    ]
    for copy in copies:
        copy.start()
    for copy in copies:
        copy.wait()


def state_kernel(k_hbm, v_hbm, s_ref, k_ref, v_ref, sems):
    fetch((k_hbm, v_hbm), (k_ref, v_ref), sems)
    for h in range(4):
        cols = slice(h * HD, (h + 1) * HD)
        s = lax.dot_general(k_ref[:, cols], v_ref[:, cols], TN, preferred_element_type=F32)
        s_ref[cols, :] = s.astype(BF16)


def states(keys, values):
    return pl.pallas_call(
        state_kernel,
        in_specs=[HBM] * 2,
        out_specs=VMEM,
        out_shape=shape(4 * HD, HD),
        scratch_shapes=[pltpu.VMEM((512, 512), BF16)] * 2 + [pltpu.SemaphoreType.DMA((2,))],
        compiler_params=pltpu.CompilerParams(vmem_limit_bytes=56 * MIB),
        cost_estimate=pl.CostEstimate(flops=2**26, bytes_accessed=MIB, transcendentals=0),
    )(keys, values)


def attention_kernel(q_hbm, k_hbm, v_hbm, c_ref, o_ref, q_ref, k_ref, v_ref, sems):
    fetch((q_hbm, k_hbm, v_hbm), (q_ref, k_ref, v_ref), sems)
    half = 256
    row = lax.broadcasted_iota(jnp.int32, (half, half), 0)
    col = lax.broadcasted_iota(jnp.int32, (half, half), 1)
    causal = row >= col

    def masked(q, k):
        s = lax.dot_general(q, k, NT, preferred_element_type=F32)
        return jnp.where(causal, s, 0.0).astype(BF16)

    def norm(a):
        r = lax.rsqrt(jnp.mean(a * a, axis=-1, keepdims=True) + 1e-06)
        return (a * r).astype(BF16)

    for h in range(4):
        cols = slice(h * HD, (h + 1) * HD)
        c = c_ref[cols]
        q0, q1 = q_ref[:half, cols], q_ref[half:, cols]
        k0, k1 = k_ref[:half, cols], k_ref[half:, cols]
        v0, v1 = v_ref[:half, cols], v_ref[half:, cols]
        a0 = jnp.dot(q0, c, preferred_element_type=F32)
        a0 += jnp.dot(masked(q0, k0), v0, preferred_element_type=F32)
        o_ref[:half, cols] = norm(a0)
        a1 = jnp.dot(q1, c, preferred_element_type=F32)
        s10 = lax.dot_general(q1, k0, NT, preferred_element_type=F32).astype(BF16)
        a1 += jnp.dot(s10, v0, preferred_element_type=F32)
        a1 += jnp.dot(masked(q1, k1), v1, preferred_element_type=F32)
        o_ref[half:, cols] = norm(a1)


def attention(queries, keys, values, carried):
    return pl.pallas_call(
        attention_kernel,
        in_specs=[HBM] * 3 + [VMEM],
        out_specs=VMEM,
        out_shape=shape(512, 512),
        scratch_shapes=[pltpu.VMEM((512, 512), BF16)] * 3 + [pltpu.SemaphoreType.DMA((3,))],
        compiler_params=pltpu.CompilerParams(vmem_limit_bytes=56 * MIB),
        cost_estimate=pl.CostEstimate(flops=2**29, bytes_accessed=2 * MIB, transcendentals=2048),
    )(queries, keys, values, carried)


def tile(n, w, z):
    w = jnp.concatenate([w[z, c, x] for x in range(X) for c in range(C)], axis=0)
    return lax.dot_general(n, w, NT, preferred_element_type=F32).astype(BF16)


def project_kernel(n_ref, w_hbm, o_hbm, w_buf, o_buf, in_sems, out_sems):
    pairs = range(MAIN // 2)
    incoming = []
    for i in pairs:
        two = pl.ds(2 * i, 2)
        incoming.append(pltpu.make_async_copy(w_hbm.at[two], w_buf.at[two], in_sems.at[i]))
        incoming[i].start()
    n = n_ref[...]
    outgoing = []
    for z in range(MAIN):
        if z % 2 == 0:
            incoming[z // 2].wait()
        cols = slice(z * 512, (z + 1) * 512)
        o_buf[:, cols] = tile(n, w_buf, z)
        copy = pltpu.make_async_copy(o_buf.at[:, cols], o_hbm.at[:, cols], out_sems.at[z])
        copy.start()
        outgoing.append(copy)
    for copy in outgoing:
        copy.wait()


def project(normed, weight):
    return pl.pallas_call(
        project_kernel,
        in_specs=[VMEM, HBM],
        out_specs=HBM,
        out_shape=shape(512, MAIN * 512),
        scratch_shapes=[
            pltpu.VMEM((MAIN, C, X, 64, 512), BF16),
            pltpu.VMEM((512, MAIN * 512), BF16),
            pltpu.SemaphoreType.DMA((MAIN // 2,)),
            pltpu.SemaphoreType.DMA((MAIN,)),
        ],
        compiler_params=pltpu.CompilerParams(vmem_limit_bytes=56 * MIB),
        cost_estimate=pl.CostEstimate(flops=2**31, bytes_accessed=6 * MIB, transcendentals=0),
    )(normed, weight)


def side_kernel(y_ref, n_ref, w_ref, up_ref, down_ref, *refs):
    starts = [pl.multiple_of(lax.rem(y_ref[0] + s, Y) * 64, 64) for s in SHIFTS]
    n = jnp.concatenate([n_ref[pl.ds(at, 64), :] for at in starts], axis=0)
    for z in range(SIDE):
        o = tile(n, w_ref, z)
        (up_ref if z < SIDE // 2 else down_ref)[...] = o[:64]
        for i, ref in enumerate(refs):
            ref[:, z * 512 : (z + 1) * 512] = o[(i + 1) * 64 : (i + 2) * 64]


def half_step_kernel(u_ref, up_ref, d_ref, down_ref, uo_ref, do_ref):
    half = up_ref.shape[1]
    uo_ref[:, :half] = add(u_ref[:, :half], up_ref[...])
    uo_ref[:, half:] = u_ref[:, half:]
    do_ref[:, :half] = d_ref[:, :half]
    do_ref[:, half:] = add(d_ref[:, half:], down_ref[...])


def step_kernel(u_ref, up_ref, d_ref, down_ref, uo_ref, do_ref):
    uo_ref[...] = add(u_ref[...], up_ref[...])
    do_ref[...] = add(d_ref[...], down_ref[...])


def add(a, b):
    return (a.astype(F32) + b.astype(F32)).astype(BF16)


def ring(up, down):
    up = lax.ppermute(up, "tp", [(i, (i + 1) % Y) for i in range(Y)])
    down = lax.ppermute(down, "tp", [(i, (i - 1) % Y) for i in range(Y)])
    return lax.optimization_barrier((up, down))


def ring_sum(y, normed, weight):
    wide, half = shape(64, SIDE * 512), shape(64, SIDE * 256)
    up, down, u3, d3, u2, d2, u1, d1, mine = call(
        side_kernel, (half, half) + (wide,) * 7, (y, normed, weight), 2**29, 3 * MIB, 1, vmem=16
    )
    up, down = ring(up, down)
    for kernel, u, d in ((half_step_kernel, u3, d3), (step_kernel, u2, d2), (step_kernel, u1, d1)):
        up, down = call(kernel, (wide, wide), (u, up, d, down), 2**18, MIB, vmem=8)
        up, down = ring(up, down)
    return (mine.astype(F32) + up.astype(F32) + down.astype(F32)).astype(BF16)


def shape(*dims, dtype=BF16):
    return jax.ShapeDtypeStruct(dims, dtype)


def everywhere(part, axis, size):
    return lax.all_to_all(jnp.broadcast_to(part[None], (size,) + part.shape), axis, 0, 0)


def on_device(queries, keys, values, out_weight):
    plane = ("x", "core")
    w_x = everywhere(out_weight.T, "x", X)
    w_x, keys = lax.optimization_barrier((w_x, keys))
    weight = lax.all_gather(w_x.reshape(X * 64, 512), ("z", "core"), axis=0, tiled=True)
    weight = weight.reshape(Z, C, X, 64, 512)

    state = states(keys, values).reshape(8, 64, HD)
    pieces = lax.all_to_all(state, plane, 0, 0)
    earlier, total = call(
        plane_kernel, (shape(8, 64, HD, dtype=F32), shape(8, 64, HD)), (pieces,), 2**17, 2**19, vmem=8
    )
    totals = lax.all_to_all(total, "z", 0, 0)
    z = lax.axis_index("z").astype(jnp.int32)[None]
    carried = call(carry_kernel, shape(8, 64, HD), (z, totals, earlier), 2**18, 2**19, 1, vmem=8)
    carried = lax.all_to_all(carried, plane, 0, 0).reshape(4 * HD, HD)

    normed = attention(queries, keys, values, carried)
    terms = project(normed, weight)
    summed = lax.psum_scatter(terms, "tp", scatter_dimension=0, tiled=True)
    side_weight, _ = lax.optimization_barrier((weight[MAIN:], terms))
    y = lax.axis_index("tp").astype(jnp.int32)[None]
    side = ring_sum(y, normed, side_weight)
    return jnp.concatenate([summed, side], axis=1)


def solution(mesh):
    split = Mesh(mesh.devices.reshape(Z, X, C, Y), ("z", "x", "core", "tp"))
    ctx = ("z", "x", "core")
    placed = (P(ctx, "tp"), P(ctx, "tp"), P(ctx, "tp"), P("tp", ctx))
    return jax.shard_map(
        on_device, mesh=split, in_specs=placed, out_specs=P((*ctx, "tp"), None), check_vma=False
    )
```

```python
import jax
import jax.numpy as jnp
from jax import lax
from jax.experimental import pallas as pl
from jax.experimental.pallas import tpu as pltpu
from jax.sharding import Mesh, PartitionSpec as P

HD = 128
F32 = jnp.float32
BF16 = jnp.bfloat16
Z, X, C, Y = 8, 4, 2, 8
MAIN, SIDE = 5, 3
SHIFTS = (4, 3, 5, 2, 6, 1, 7, 0)
MIB = 2**20
NT = (((1,), (1,)), ((), ()))
TN = (((0,), (0,)), ((), ()))
VMEM = pl.BlockSpec(memory_space=pltpu.VMEM)
SMEM = pl.BlockSpec(memory_space=pltpu.SMEM)
HBM = pl.BlockSpec(memory_space=pltpu.HBM)


def call(kernel, out_shape, operands, flops, moved, scalars=0, vmem=24):
    return pl.pallas_call(
        kernel,
        out_shape=out_shape,
        in_specs=[SMEM] * scalars + [VMEM] * (len(operands) - scalars),
        out_specs=jax.tree.map(lambda _: VMEM, out_shape),
        compiler_params=pltpu.CompilerParams(vmem_limit_bytes=vmem * MIB),
        cost_estimate=pl.CostEstimate(flops=flops, bytes_accessed=moved, transcendentals=0),
    )(*operands)


def plane_kernel(p_ref, e_ref, t_ref):
    running = jnp.zeros(p_ref.shape[1:], F32)
    for i in range(C * X):
        e_ref[i] = running
        running = running + p_ref[i].astype(F32)
    total = running.astype(BF16)
    for i in range(Z):
        t_ref[i] = total


def carry_kernel(z_ref, t_ref, e_ref, c_ref):
    z = z_ref[0]
    before = jnp.zeros(t_ref.shape[1:], F32)
    for i in range(Z - 1):
        before = before + jnp.where(i < z, t_ref[i].astype(F32), 0.0)
    for i in range(C * X):
        c_ref[i] = (e_ref[i] + before).astype(BF16)


def fetch(sources, buffers, sems):
    copies = [
        pltpu.make_async_copy(source, buffer, sems.at[i])
        for i, (source, buffer) in enumerate(zip(sources, buffers))
    ]
    for copy in copies:
        copy.start()
    for copy in copies:
        copy.wait()


def state_kernel(k_hbm, v_hbm, s_ref, k_ref, v_ref, sems):
    fetch((k_hbm, v_hbm), (k_ref, v_ref), sems)
    for h in range(4):
        cols = slice(h * HD, (h + 1) * HD)
        s = lax.dot_general(k_ref[:, cols], v_ref[:, cols], TN, preferred_element_type=F32)
        s_ref[cols, :] = s.astype(BF16)


def states(keys, values):
    return pl.pallas_call(
        state_kernel,
        in_specs=[HBM] * 2,
        out_specs=VMEM,
        out_shape=shape(4 * HD, HD),
        scratch_shapes=[pltpu.VMEM((512, 512), BF16)] * 2 + [pltpu.SemaphoreType.DMA((2,))],
        compiler_params=pltpu.CompilerParams(vmem_limit_bytes=56 * MIB),
        cost_estimate=pl.CostEstimate(flops=2**26, bytes_accessed=MIB, transcendentals=0),
    )(keys, values)


def attention_kernel(q_hbm, k_hbm, v_hbm, c_ref, o_ref, q_ref, k_ref, v_ref, sems):
    fetch((q_hbm, k_hbm, v_hbm), (q_ref, k_ref, v_ref), sems)
    half = 256
    row = lax.broadcasted_iota(jnp.int32, (half, half), 0)
    col = lax.broadcasted_iota(jnp.int32, (half, half), 1)
    causal = row >= col

    def masked(q, k):
        s = lax.dot_general(q, k, NT, preferred_element_type=F32)
        return jnp.where(causal, s, 0.0).astype(BF16)

    def norm(a):
        r = lax.rsqrt(jnp.mean(a * a, axis=-1, keepdims=True) + 1e-06)
        return (a * r).astype(BF16)

    for h in range(4):
        cols = slice(h * HD, (h + 1) * HD)
        c = c_ref[cols]
        q0, q1 = q_ref[:half, cols], q_ref[half:, cols]
        k0, k1 = k_ref[:half, cols], k_ref[half:, cols]
        v0, v1 = v_ref[:half, cols], v_ref[half:, cols]
        a0 = jnp.dot(q0, c, preferred_element_type=F32)
        a0 += jnp.dot(masked(q0, k0), v0, preferred_element_type=F32)
        o_ref[:half, cols] = norm(a0)
        a1 = jnp.dot(q1, c, preferred_element_type=F32)
        s10 = lax.dot_general(q1, k0, NT, preferred_element_type=F32).astype(BF16)
        a1 += jnp.dot(s10, v0, preferred_element_type=F32)
        a1 += jnp.dot(masked(q1, k1), v1, preferred_element_type=F32)
        o_ref[half:, cols] = norm(a1)


def attention(queries, keys, values, carried):
    return pl.pallas_call(
        attention_kernel,
        in_specs=[HBM] * 3 + [VMEM],
        out_specs=VMEM,
        out_shape=shape(512, 512),
        scratch_shapes=[pltpu.VMEM((512, 512), BF16)] * 3 + [pltpu.SemaphoreType.DMA((3,))],
        compiler_params=pltpu.CompilerParams(vmem_limit_bytes=56 * MIB),
        cost_estimate=pl.CostEstimate(flops=2**29, bytes_accessed=2 * MIB, transcendentals=2048),
    )(queries, keys, values, carried)


def tile(n, w, z):
    w = jnp.concatenate([w[z, c, x] for x in range(X) for c in range(C)], axis=0)
    return lax.dot_general(n, w, NT, preferred_element_type=F32).astype(BF16)


def project_kernel(n_ref, w_hbm, o_hbm, w_buf, o_buf, in_sems, out_sems):
    incoming = {}
    for i, z in enumerate(range(0, MAIN, 2)):
        some = pl.ds(z, min(2, MAIN - z))
        incoming[z] = pltpu.make_async_copy(w_hbm.at[some], w_buf.at[some], in_sems.at[i])
        incoming[z].start()
    n = n_ref[...]
    outgoing = []
    for z in range(MAIN):
        if z in incoming:
            incoming[z].wait()
        cols = slice(z * 512, (z + 1) * 512)
        o_buf[:, cols] = tile(n, w_buf, z)
        copy = pltpu.make_async_copy(o_buf.at[:, cols], o_hbm.at[:, cols], out_sems.at[z])
        copy.start()
        outgoing.append(copy)
    for copy in outgoing:
        copy.wait()


def project(normed, weight):
    return pl.pallas_call(
        project_kernel,
        in_specs=[VMEM, HBM],
        out_specs=HBM,
        out_shape=shape(512, MAIN * 512),
        scratch_shapes=[
            pltpu.VMEM((MAIN, C, X, 64, 512), BF16),
            pltpu.VMEM((512, MAIN * 512), BF16),
            pltpu.SemaphoreType.DMA((-(-MAIN // 2),)),
            pltpu.SemaphoreType.DMA((MAIN,)),
        ],
        compiler_params=pltpu.CompilerParams(vmem_limit_bytes=56 * MIB),
        cost_estimate=pl.CostEstimate(flops=2**31, bytes_accessed=6 * MIB, transcendentals=0),
    )(normed, weight)


def side_kernel(y_ref, n_ref, w_ref, up_ref, down_ref, *refs):
    starts = [pl.multiple_of(lax.rem(y_ref[0] + s, Y) * 64, 64) for s in SHIFTS]
    n = jnp.concatenate([n_ref[pl.ds(at, 64), :] for at in starts], axis=0)
    for z in range(SIDE):
        o = tile(n, w_ref, z)
        for at in (0, 256):
            side, to = divmod(z * 512 + at, SIDE * 256)
            (up_ref, down_ref)[side][:, to : to + 256] = o[:64, at : at + 256]
        for i, ref in enumerate(refs):
            ref[:, z * 512 : (z + 1) * 512] = o[(i + 1) * 64 : (i + 2) * 64]


def half_step_kernel(u_ref, up_ref, d_ref, down_ref, uo_ref, do_ref):
    half = up_ref.shape[1]
    uo_ref[:, :half] = add(u_ref[:, :half], up_ref[...])
    uo_ref[:, half:] = u_ref[:, half:]
    do_ref[:, :half] = d_ref[:, :half]
    do_ref[:, half:] = add(d_ref[:, half:], down_ref[...])


def step_kernel(u_ref, up_ref, d_ref, down_ref, uo_ref, do_ref):
    uo_ref[...] = add(u_ref[...], up_ref[...])
    do_ref[...] = add(d_ref[...], down_ref[...])


def add(a, b):
    return (a.astype(F32) + b.astype(F32)).astype(BF16)


def ring(up, down):
    up = lax.ppermute(up, "tp", [(i, (i + 1) % Y) for i in range(Y)])
    down = lax.ppermute(down, "tp", [(i, (i - 1) % Y) for i in range(Y)])
    return lax.optimization_barrier((up, down))


def ring_sum(y, normed, weight):
    wide, half = shape(64, SIDE * 512), shape(64, SIDE * 256)
    up, down, u3, d3, u2, d2, u1, d1, mine = call(
        side_kernel, (half, half) + (wide,) * 7, (y, normed, weight), 2**29, 3 * MIB, 1, vmem=16
    )
    up, down = ring(up, down)
    for kernel, u, d in ((half_step_kernel, u3, d3), (step_kernel, u2, d2), (step_kernel, u1, d1)):
        up, down = call(kernel, (wide, wide), (u, up, d, down), 2**18, MIB, vmem=8)
        up, down = ring(up, down)
    return (mine.astype(F32) + up.astype(F32) + down.astype(F32)).astype(BF16)


def shape(*dims, dtype=BF16):
    return jax.ShapeDtypeStruct(dims, dtype)


def everywhere(part, axis, size):
    return lax.all_to_all(jnp.broadcast_to(part[None], (size,) + part.shape), axis, 0, 0)


def on_device(queries, keys, values, out_weight):
    plane = ("x", "core")
    w_x = everywhere(out_weight.T, "x", X)
    w_x, keys = lax.optimization_barrier((w_x, keys))
    weight = lax.all_gather(w_x.reshape(X * 64, 512), ("z", "core"), axis=0, tiled=True)
    weight = weight.reshape(Z, C, X, 64, 512)

    state = states(keys, values).reshape(8, 64, HD)
    pieces = lax.all_to_all(state, plane, 0, 0)
    earlier, total = call(
        plane_kernel, (shape(8, 64, HD, dtype=F32), shape(8, 64, HD)), (pieces,), 2**17, 2**19, vmem=8
    )
    totals = lax.all_to_all(total, "z", 0, 0)
    z = lax.axis_index("z").astype(jnp.int32)[None]
    carried = call(carry_kernel, shape(8, 64, HD), (z, totals, earlier), 2**18, 2**19, 1, vmem=8)
    carried = lax.all_to_all(carried, plane, 0, 0).reshape(4 * HD, HD)

    normed = attention(queries, keys, values, carried)
    terms = project(normed, weight)
    summed = lax.psum_scatter(terms, "tp", scatter_dimension=0, tiled=True)
    side_weight, _ = lax.optimization_barrier((weight[MAIN:], terms))
    y = lax.axis_index("tp").astype(jnp.int32)[None]
    side = ring_sum(y, normed, side_weight)
    return jnp.concatenate([summed, side], axis=1)


def solution(mesh):
    split = Mesh(mesh.devices.reshape(Z, X, C, Y), ("z", "x", "core", "tp"))
    ctx = ("z", "x", "core")
    placed = (P(ctx, "tp"), P(ctx, "tp"), P(ctx, "tp"), P("tp", ctx))
    return jax.shard_map(
        on_device, mesh=split, in_specs=placed, out_specs=P((*ctx, "tp"), None), check_vma=False
    )
```

```python
import jax
import jax.numpy as jnp
from jax import lax
from jax.experimental import pallas as pl
from jax.experimental.pallas import tpu as pltpu
from jax.sharding import Mesh, PartitionSpec as P

HD = 128
F32 = jnp.float32
BF16 = jnp.bfloat16
Z, X, C, Y = 8, 4, 2, 8
MAIN, SIDE = 5, 3
MIB = 2**20
NT = (((1,), (1,)), ((), ()))
TN = (((0,), (0,)), ((), ()))
VMEM = pl.BlockSpec(memory_space=pltpu.VMEM)
SMEM = pl.BlockSpec(memory_space=pltpu.SMEM)
HBM = pl.BlockSpec(memory_space=pltpu.HBM)


def call(kernel, out_shape, operands, flops, moved, scalars=0, vmem=24):
    return pl.pallas_call(
        kernel,
        out_shape=out_shape,
        in_specs=[SMEM] * scalars + [VMEM] * (len(operands) - scalars),
        out_specs=jax.tree.map(lambda _: VMEM, out_shape),
        compiler_params=pltpu.CompilerParams(vmem_limit_bytes=vmem * MIB),
        cost_estimate=pl.CostEstimate(flops=flops, bytes_accessed=moved, transcendentals=0),
    )(*operands)


def plane_kernel(p_ref, e_ref, t_ref):
    running = jnp.zeros(p_ref.shape[1:], F32)
    for i in range(C * X):
        e_ref[i] = running
        running = running + p_ref[i].astype(F32)
    total = running.astype(BF16)
    for i in range(Z):
        t_ref[i] = total


def carry_kernel(z_ref, t_ref, e_ref, c_ref):
    z = z_ref[0]
    before = jnp.zeros(t_ref.shape[1:], F32)
    for i in range(Z - 1):
        before = before + jnp.where(i < z, t_ref[i].astype(F32), 0.0)
    for i in range(C * X):
        c_ref[i] = (e_ref[i] + before).astype(BF16)


def fetch(sources, buffers, sems):
    copies = [
        pltpu.make_async_copy(source, buffer, sems.at[i])
        for i, (source, buffer) in enumerate(zip(sources, buffers))
    ]
    for copy in copies:
        copy.start()
    for copy in copies:
        copy.wait()


def state_kernel(k_hbm, v_hbm, s_ref, k_ref, v_ref, sems):
    fetch((k_hbm, v_hbm), (k_ref, v_ref), sems)
    for h in range(4):
        cols = slice(h * HD, (h + 1) * HD)
        s = lax.dot_general(k_ref[:, cols], v_ref[:, cols], TN, preferred_element_type=F32)
        s_ref[cols, :] = s.astype(BF16)


def states(keys, values):
    return pl.pallas_call(
        state_kernel,
        in_specs=[HBM] * 2,
        out_specs=VMEM,
        out_shape=shape(4 * HD, HD),
        scratch_shapes=[pltpu.VMEM((512, 512), BF16)] * 2 + [pltpu.SemaphoreType.DMA((2,))],
        compiler_params=pltpu.CompilerParams(vmem_limit_bytes=56 * MIB),
        cost_estimate=pl.CostEstimate(flops=2**26, bytes_accessed=MIB, transcendentals=0),
    )(keys, values)


def attention_kernel(q_hbm, k_hbm, v_hbm, c_ref, o_ref, q_ref, k_ref, v_ref, sems):
    fetch((q_hbm, k_hbm, v_hbm), (q_ref, k_ref, v_ref), sems)
    half = 256
    row = lax.broadcasted_iota(jnp.int32, (half, half), 0)
    col = lax.broadcasted_iota(jnp.int32, (half, half), 1)
    causal = row >= col

    def masked(q, k):
        s = lax.dot_general(q, k, NT, preferred_element_type=F32)
        return jnp.where(causal, s, 0.0).astype(BF16)

    def norm(a):
        r = lax.rsqrt(jnp.mean(a * a, axis=-1, keepdims=True) + 1e-06)
        return (a * r).astype(BF16)

    for h in range(4):
        cols = slice(h * HD, (h + 1) * HD)
        c = c_ref[cols]
        q0, q1 = q_ref[:half, cols], q_ref[half:, cols]
        k0, k1 = k_ref[:half, cols], k_ref[half:, cols]
        v0, v1 = v_ref[:half, cols], v_ref[half:, cols]
        a0 = jnp.dot(q0, c, preferred_element_type=F32)
        a0 += jnp.dot(masked(q0, k0), v0, preferred_element_type=F32)
        o_ref[:half, cols] = norm(a0)
        a1 = jnp.dot(q1, c, preferred_element_type=F32)
        s10 = lax.dot_general(q1, k0, NT, preferred_element_type=F32).astype(BF16)
        a1 += jnp.dot(s10, v0, preferred_element_type=F32)
        a1 += jnp.dot(masked(q1, k1), v1, preferred_element_type=F32)
        o_ref[half:, cols] = norm(a1)


def attention(queries, keys, values, carried):
    return pl.pallas_call(
        attention_kernel,
        in_specs=[HBM] * 3 + [VMEM],
        out_specs=VMEM,
        out_shape=shape(512, 512),
        scratch_shapes=[pltpu.VMEM((512, 512), BF16)] * 3 + [pltpu.SemaphoreType.DMA((3,))],
        compiler_params=pltpu.CompilerParams(vmem_limit_bytes=56 * MIB),
        cost_estimate=pl.CostEstimate(flops=2**29, bytes_accessed=2 * MIB, transcendentals=2048),
    )(queries, keys, values, carried)


def tile(n, w, z):
    w = jnp.concatenate([w[z, c, x] for x in range(X) for c in range(C)], axis=0)
    return lax.dot_general(n, w, NT, preferred_element_type=F32).astype(BF16)


def project_kernel(n_ref, w_hbm, o_hbm, w_buf, o_buf, in_sems, out_sems):
    incoming = {}
    for i, z in enumerate(range(0, MAIN, 2)):
        some = pl.ds(z, min(2, MAIN - z))
        incoming[z] = pltpu.make_async_copy(w_hbm.at[some], w_buf.at[some], in_sems.at[i])
        incoming[z].start()
    n = n_ref[...]
    outgoing = []
    for z in range(MAIN):
        if z in incoming:
            incoming[z].wait()
        cols = slice(z * 512, (z + 1) * 512)
        o_buf[:, cols] = tile(n, w_buf, z)
        copy = pltpu.make_async_copy(o_buf.at[:, cols], o_hbm.at[:, cols], out_sems.at[z])
        copy.start()
        outgoing.append(copy)
    for copy in outgoing:
        copy.wait()


def project(normed, weight):
    return pl.pallas_call(
        project_kernel,
        in_specs=[VMEM, HBM],
        out_specs=HBM,
        out_shape=shape(512, MAIN * 512),
        scratch_shapes=[
            pltpu.VMEM((MAIN, C, X, 64, 512), BF16),
            pltpu.VMEM((512, MAIN * 512), BF16),
            pltpu.SemaphoreType.DMA((-(-MAIN // 2),)),
            pltpu.SemaphoreType.DMA((MAIN,)),
        ],
        compiler_params=pltpu.CompilerParams(vmem_limit_bytes=56 * MIB),
        cost_estimate=pl.CostEstimate(flops=2**31, bytes_accessed=6 * MIB, transcendentals=0),
    )(normed, weight)


def pair(own, other, core):
    return jnp.where(core == 0, own, other), jnp.where(core == 0, other, own)


def side_kernel(place_ref, n_ref, m_ref, w_ref, first_ref, *refs):
    y, core = place_ref[0], place_ref[1]
    shifts = [4] + [jnp.where(core == 0, 3 - i, 5 + i) for i in range(3)]
    rows = []
    for shift in shifts:
        at = pl.ds(pl.multiple_of(lax.rem(y + shift, Y) * 64, 64), 64)
        rows += pair(n_ref[at, :], m_ref[at, :], core)
    rows.append(n_ref[pl.ds(pl.multiple_of(y * 64, 64), 64), :])
    n = jnp.concatenate(rows, axis=0)
    for z in range(SIDE):
        o = tile(n, w_ref, z)
        for at in (0, 256):
            side, to = divmod(z * 512 + at, SIDE * 256)

            @pl.when(core == side)
            def _(to=to, piece=o[:128, at : at + 256]):
                first_ref[:, to : to + 256] = piece

        cols = slice(z * 512, (z + 1) * 512)
        for i, ref in enumerate(refs):
            ref[:, cols] = o[(i + 1) * 128 : (i + 1) * 128 + ref.shape[0]]


def half_step_kernel(core_ref, p_ref, r_ref, o_ref):
    half = r_ref.shape[1]
    for side in range(C):
        cols = slice(side * half, (side + 1) * half)
        more = jnp.where(core_ref[0] == side, r_ref[...].astype(F32), 0.0)
        o_ref[:, cols] = (p_ref[:, cols].astype(F32) + more).astype(BF16)


def step_kernel(p_ref, r_ref, o_ref):
    o_ref[...] = add(p_ref[...], r_ref[...])


def split_kernel(core_ref, r_ref, keep_ref, send_ref):
    keep_ref[...], send_ref[...] = pair(r_ref[:64], r_ref[64:], core_ref[0])


def add(a, b):
    return (a.astype(F32) + b.astype(F32)).astype(BF16)


def ring(part):
    up = [(i, (i + 1) % Y) for i in range(Y)]
    down = [(Y + i, Y + (i - 1) % Y) for i in range(Y)]
    return lax.ppermute(part, ("core", "tp"), up + down)


def ring_sum(y, core, normed, swapped, weight):
    wide, half, mine = shape(128, SIDE * 512), shape(128, SIDE * 256), shape(64, SIDE * 512)
    place = jnp.concatenate([y, core])
    part, p3, p2, p1, mine = call(
        side_kernel, (half, wide, wide, wide, mine), (place, normed, swapped, weight), 2**29, 3 * MIB, 1, vmem=16
    )
    part = call(half_step_kernel, wide, (core, p3, ring(part)), 2**18, MIB, 1, vmem=8)
    part = call(step_kernel, wide, (p2, ring(part)), 2**18, MIB, vmem=8)
    part = call(step_kernel, wide, (p1, ring(part)), 2**18, MIB, vmem=8)
    size = shape(64, SIDE * 512)
    keep, send = call(split_kernel, (size, size), (core, ring(part)), 2**18, MIB, 1, vmem=8)
    got = lax.ppermute(send, "core", [(0, 1), (1, 0)])
    return (mine.astype(F32) + keep.astype(F32) + got.astype(F32)).astype(BF16)


def shape(*dims, dtype=BF16):
    return jax.ShapeDtypeStruct(dims, dtype)


def everywhere(part, axis, size):
    return lax.all_to_all(jnp.broadcast_to(part[None], (size,) + part.shape), axis, 0, 0)


def on_device(queries, keys, values, out_weight):
    plane = ("x", "core")
    w_x = everywhere(out_weight.T, "x", X)
    w_x, keys = lax.optimization_barrier((w_x, keys))
    weight = lax.all_gather(w_x.reshape(X * 64, 512), ("z", "core"), axis=0, tiled=True)
    weight = weight.reshape(Z, C, X, 64, 512)

    state = states(keys, values).reshape(8, 64, HD)
    pieces = lax.all_to_all(state, plane, 0, 0)
    earlier, total = call(
        plane_kernel, (shape(8, 64, HD, dtype=F32), shape(8, 64, HD)), (pieces,), 2**17, 2**19, vmem=8
    )
    totals = lax.all_to_all(total, "z", 0, 0)
    z = lax.axis_index("z").astype(jnp.int32)[None]
    carried = call(carry_kernel, shape(8, 64, HD), (z, totals, earlier), 2**18, 2**19, 1, vmem=8)
    carried = lax.all_to_all(carried, plane, 0, 0).reshape(4 * HD, HD)

    normed = attention(queries, keys, values, carried)
    swapped = lax.ppermute(normed, "core", [(0, 1), (1, 0)])
    swapped, main = lax.optimization_barrier((swapped, normed))
    terms = project(main, weight)
    summed = lax.psum_scatter(terms, "tp", scatter_dimension=0, tiled=True)
    side_weight, _ = lax.optimization_barrier((weight[MAIN:], terms))
    y = lax.axis_index("tp").astype(jnp.int32)[None]
    core = lax.axis_index("core").astype(jnp.int32)[None]
    side = ring_sum(y, core, normed, swapped, side_weight)
    return jnp.concatenate([summed, side], axis=1)


def solution(mesh):
    split = Mesh(mesh.devices.reshape(Z, X, C, Y), ("z", "x", "core", "tp"))
    ctx = ("z", "x", "core")
    placed = (P(ctx, "tp"), P(ctx, "tp"), P(ctx, "tp"), P("tp", ctx))
    return jax.shard_map(
        on_device, mesh=split, in_specs=placed, out_specs=P((*ctx, "tp"), None), check_vma=False
    )
```

```python
import jax
import jax.numpy as jnp
from jax import lax
from jax.experimental import pallas as pl
from jax.experimental.pallas import tpu as pltpu
from jax.sharding import Mesh, PartitionSpec as P

HD = 128
F32 = jnp.float32
BF16 = jnp.bfloat16
Z, X, C, Y = 8, 4, 2, 8
MAIN, SIDE = 6, 2
SHIFTS = (4, 3, 5, 2, 6, 1, 7, 0)
MIB = 2**20
NT = (((1,), (1,)), ((), ()))
TN = (((0,), (0,)), ((), ()))
VMEM = pl.BlockSpec(memory_space=pltpu.VMEM)
SMEM = pl.BlockSpec(memory_space=pltpu.SMEM)
HBM = pl.BlockSpec(memory_space=pltpu.HBM)


def call(kernel, out_shape, operands, flops, moved, scalars=0, vmem=24):
    return pl.pallas_call(
        kernel,
        out_shape=out_shape,
        in_specs=[SMEM] * scalars + [VMEM] * (len(operands) - scalars),
        out_specs=jax.tree.map(lambda _: VMEM, out_shape),
        compiler_params=pltpu.CompilerParams(vmem_limit_bytes=vmem * MIB),
        cost_estimate=pl.CostEstimate(flops=flops, bytes_accessed=moved, transcendentals=0),
    )(*operands)


def plane_kernel(p_ref, e_ref, t_ref):
    running = jnp.zeros(p_ref.shape[1:], F32)
    for i in range(C * X):
        e_ref[i] = running
        running = running + p_ref[i].astype(F32)
    total = running.astype(BF16)
    for i in range(Z):
        t_ref[i] = total


def carry_kernel(z_ref, t_ref, e_ref, c_ref):
    z = z_ref[0]
    before = jnp.zeros(t_ref.shape[1:], F32)
    for i in range(Z - 1):
        before = before + jnp.where(i < z, t_ref[i].astype(F32), 0.0)
    for i in range(C * X):
        c_ref[i] = (e_ref[i] + before).astype(BF16)


def fetch(sources, buffers, sems):
    copies = [
        pltpu.make_async_copy(source, buffer, sems.at[i])
        for i, (source, buffer) in enumerate(zip(sources, buffers))
    ]
    for copy in copies:
        copy.start()
    for copy in copies:
        copy.wait()


def state_kernel(k_hbm, v_hbm, s_ref, k_ref, v_ref, sems):
    fetch((k_hbm, v_hbm), (k_ref, v_ref), sems)
    for h in range(4):
        cols = slice(h * HD, (h + 1) * HD)
        s = lax.dot_general(k_ref[:, cols], v_ref[:, cols], TN, preferred_element_type=F32)
        s_ref[cols, :] = s.astype(BF16)


def states(keys, values):
    return pl.pallas_call(
        state_kernel,
        in_specs=[HBM] * 2,
        out_specs=VMEM,
        out_shape=shape(4 * HD, HD),
        scratch_shapes=[pltpu.VMEM((512, 512), BF16)] * 2 + [pltpu.SemaphoreType.DMA((2,))],
        compiler_params=pltpu.CompilerParams(vmem_limit_bytes=56 * MIB),
        cost_estimate=pl.CostEstimate(flops=2**26, bytes_accessed=MIB, transcendentals=0),
    )(keys, values)


def attention_kernel(q_hbm, k_hbm, v_hbm, c_ref, o_ref, q_ref, k_ref, v_ref, sems):
    fetch((q_hbm, k_hbm, v_hbm), (q_ref, k_ref, v_ref), sems)
    half = 256
    row = lax.broadcasted_iota(jnp.int32, (half, half), 0)
    col = lax.broadcasted_iota(jnp.int32, (half, half), 1)
    causal = row >= col

    def masked(q, k):
        s = lax.dot_general(q, k, NT, preferred_element_type=F32)
        return jnp.where(causal, s, 0.0).astype(BF16)

    def norm(a):
        r = lax.rsqrt(jnp.mean(a * a, axis=-1, keepdims=True) + 1e-06)
        return (a * r).astype(BF16)

    for h in range(4):
        cols = slice(h * HD, (h + 1) * HD)
        c = c_ref[cols]
        q0, q1 = q_ref[:half, cols], q_ref[half:, cols]
        k0, k1 = k_ref[:half, cols], k_ref[half:, cols]
        v0, v1 = v_ref[:half, cols], v_ref[half:, cols]
        a0 = jnp.dot(q0, c, preferred_element_type=F32)
        a0 += jnp.dot(masked(q0, k0), v0, preferred_element_type=F32)
        o_ref[:half, cols] = norm(a0)
        a1 = jnp.dot(q1, c, preferred_element_type=F32)
        s10 = lax.dot_general(q1, k0, NT, preferred_element_type=F32).astype(BF16)
        a1 += jnp.dot(s10, v0, preferred_element_type=F32)
        a1 += jnp.dot(masked(q1, k1), v1, preferred_element_type=F32)
        o_ref[half:, cols] = norm(a1)


def attention(queries, keys, values, carried):
    return pl.pallas_call(
        attention_kernel,
        in_specs=[HBM] * 3 + [VMEM],
        out_specs=VMEM,
        out_shape=shape(512, 512),
        scratch_shapes=[pltpu.VMEM((512, 512), BF16)] * 3 + [pltpu.SemaphoreType.DMA((3,))],
        compiler_params=pltpu.CompilerParams(vmem_limit_bytes=56 * MIB),
        cost_estimate=pl.CostEstimate(flops=2**29, bytes_accessed=2 * MIB, transcendentals=2048),
    )(queries, keys, values, carried)


def tile(n, w, z):
    w = jnp.concatenate([w[c, z, x] for x in range(X) for c in range(C)], axis=0)
    return lax.dot_general(n, w, NT, preferred_element_type=F32).astype(BF16)


def project_kernel(n_ref, w_hbm, o_hbm, w_buf, o_buf, in_sems, out_sems):
    pairs = range(MAIN // 2)
    incoming = []
    for i in pairs:
        two = pl.ds(2 * i, 2)
        incoming.append(pltpu.make_async_copy(w_hbm.at[:, two], w_buf.at[:, two], in_sems.at[i]))
        incoming[i].start()
    n = n_ref[...]
    outgoing = []
    for z in range(MAIN):
        if z % 2 == 0:
            incoming[z // 2].wait()
        cols = slice(z * 512, (z + 1) * 512)
        o_buf[:, cols] = tile(n, w_buf, z)
        copy = pltpu.make_async_copy(o_buf.at[:, cols], o_hbm.at[:, cols], out_sems.at[z])
        copy.start()
        outgoing.append(copy)
    for copy in outgoing:
        copy.wait()


def project(normed, weight):
    return pl.pallas_call(
        project_kernel,
        in_specs=[VMEM, HBM],
        out_specs=HBM,
        out_shape=shape(512, MAIN * 512),
        scratch_shapes=[
            pltpu.VMEM((C, MAIN, X, 64, 512), BF16),
            pltpu.VMEM((512, MAIN * 512), BF16),
            pltpu.SemaphoreType.DMA((MAIN // 2,)),
            pltpu.SemaphoreType.DMA((MAIN,)),
        ],
        compiler_params=pltpu.CompilerParams(vmem_limit_bytes=56 * MIB),
        cost_estimate=pl.CostEstimate(flops=2**31, bytes_accessed=6 * MIB, transcendentals=0),
    )(normed, weight)


def side_kernel(y_ref, n_ref, w_ref, up_ref, down_ref, *refs):
    starts = [pl.multiple_of(lax.rem(y_ref[0] + s, Y) * 64, 64) for s in SHIFTS]
    n = jnp.concatenate([n_ref[pl.ds(at, 64), :] for at in starts], axis=0)
    for z in range(SIDE):
        o = tile(n, w_ref, z)
        (up_ref if z < SIDE // 2 else down_ref)[...] = o[:64]
        for i, ref in enumerate(refs):
            ref[:, z * 512 : (z + 1) * 512] = o[(i + 1) * 64 : (i + 2) * 64]


def half_step_kernel(u_ref, up_ref, d_ref, down_ref, uo_ref, do_ref):
    half = up_ref.shape[1]
    uo_ref[:, :half] = add(u_ref[:, :half], up_ref[...])
    uo_ref[:, half:] = u_ref[:, half:]
    do_ref[:, :half] = d_ref[:, :half]
    do_ref[:, half:] = add(d_ref[:, half:], down_ref[...])


def step_kernel(u_ref, up_ref, d_ref, down_ref, uo_ref, do_ref):
    uo_ref[...] = add(u_ref[...], up_ref[...])
    do_ref[...] = add(d_ref[...], down_ref[...])


def add(a, b):
    return (a.astype(F32) + b.astype(F32)).astype(BF16)


def ring(up, down):
    up = lax.ppermute(up, "tp", [(i, (i + 1) % Y) for i in range(Y)])
    down = lax.ppermute(down, "tp", [(i, (i - 1) % Y) for i in range(Y)])
    return lax.optimization_barrier((up, down))


def ring_sum(y, normed, weight):
    wide, half = shape(64, SIDE * 512), shape(64, SIDE * 256)
    up, down, u3, d3, u2, d2, u1, d1, mine = call(
        side_kernel, (half, half) + (wide,) * 7, (y, normed, weight), 2**29, 3 * MIB, 1, vmem=16
    )
    up, down = ring(up, down)
    for kernel, u, d in ((half_step_kernel, u3, d3), (step_kernel, u2, d2), (step_kernel, u1, d1)):
        up, down = call(kernel, (wide, wide), (u, up, d, down), 2**18, MIB, vmem=8)
        up, down = ring(up, down)
    return (mine.astype(F32) + up.astype(F32) + down.astype(F32)).astype(BF16)


def shape(*dims, dtype=BF16):
    return jax.ShapeDtypeStruct(dims, dtype)


def everywhere(part, axis, size):
    return lax.all_to_all(jnp.broadcast_to(part[None], (size,) + part.shape), axis, 0, 0)


def on_device(queries, keys, values, out_weight):
    plane = ("x", "core")
    w_x = everywhere(out_weight.T, "x", X)
    w_x, keys = lax.optimization_barrier((w_x, keys))
    weight = lax.all_gather(w_x.reshape(X * 64, 512), ("core", "z"), axis=0, tiled=True)
    weight = weight.reshape(C, Z, X, 64, 512)

    state = states(keys, values).reshape(8, 64, HD)
    pieces = lax.all_to_all(state, plane, 0, 0)
    earlier, total = call(
        plane_kernel, (shape(8, 64, HD, dtype=F32), shape(8, 64, HD)), (pieces,), 2**17, 2**19, vmem=8
    )
    totals = lax.all_to_all(total, "z", 0, 0)
    z = lax.axis_index("z").astype(jnp.int32)[None]
    carried = call(carry_kernel, shape(8, 64, HD), (z, totals, earlier), 2**18, 2**19, 1, vmem=8)
    carried = lax.all_to_all(carried, plane, 0, 0).reshape(4 * HD, HD)

    normed = attention(queries, keys, values, carried)
    terms = project(normed, weight)
    summed = lax.psum_scatter(terms, "tp", scatter_dimension=0, tiled=True)
    side_weight, _ = lax.optimization_barrier((weight[:, MAIN:], terms))
    y = lax.axis_index("tp").astype(jnp.int32)[None]
    side = ring_sum(y, normed, side_weight)
    return jnp.concatenate([summed, side], axis=1)


def solution(mesh):
    split = Mesh(mesh.devices.reshape(Z, X, C, Y), ("z", "x", "core", "tp"))
    ctx = ("z", "x", "core")
    placed = (P(ctx, "tp"), P(ctx, "tp"), P(ctx, "tp"), P("tp", ctx))
    return jax.shard_map(
        on_device, mesh=split, in_specs=placed, out_specs=P((*ctx, "tp"), None), check_vma=False
    )
```
